32 devices in a mesh: row: 8 (over y, x, core), col: 4 (over z).
Axes of the slice: x: 2, y: 2, z: 4, core: 2. Of those that a mesh axis runs over, the one named last changes fastest.
Arguments:
- image: bfloat16 [256, 512, 256], P('row', 'col'), may hold values from -60 to 60
- bn_gain: float32 [256], replicated, may hold values from 0.5 to 2
- bn_shift: float32 [256], replicated, may hold values from -3 to 3
- expand_weight: bfloat16 [256, 1024], replicated, may hold values from -0.375 to 0.375
- expand_bias: float32 [1024], replicated, may hold values from -3 to 3
- depth_kernel: bfloat16 [3, 3, 1024], replicated, may hold values from -2 to 2
- depth_bias: float32 [1024], replicated, may hold values from -3 to 3
- project_weight: bfloat16 [1024, 256], replicated, may hold values from -0.1875 to 0.1875
- norm_gain: float32 [2, 256], replicated, may hold values from 0.5 to 2
- qkv_weight: bfloat16 [2, 256, 768], replicated, may hold values from -7 to 7
- out_weight: bfloat16 [2, 256, 256], replicated, may hold values from -0.375 to 0.375
Outputs:
- features_out: bfloat16 [256, 512, 256], P('row', 'col')
The draws below stay inside these ranges and needn't reach their ends.
All inputs are finite; a program needn't handle non-finite values.
Results may differ from the reference program's by a relative error of at most 0.011.
Values may be sent and summed in bfloat16 or wider, within the bound.
A program may use at most 128 MiB of HBM per device.

```python
import math
import jax
import jax.numpy as jnp
from jax import lax

CHANNELS = 256
HEADS = 8
HIDDEN_CH = 1024
WINDOW = 8
GRID_SIDE = 16
GRID_ROWS = 256
GRID_COLS = 512


def draw_image(key, part):
    key = jax.random.fold_in(key, 11)
    keys = jax.random.split(key, 1)
    field = jnp.clip(jax.random.normal(keys[0], (GRID_ROWS, GRID_COLS, CHANNELS), jnp.float32), -6.0, 6.0)
    return field.astype(jnp.bfloat16)


def draw_qkv_weight(key, part):
    key = jax.random.fold_in(key, 23)
    keys = jax.random.split(key, 1)
    base = jnp.clip(jax.random.normal(keys[0], (2, CHANNELS, 3 * CHANNELS), jnp.float32), -5.0, 5.0) / math.sqrt(CHANNELS)
    return base.astype(jnp.bfloat16)


def gaussian(key, shape, width, bound, dtype=jnp.bfloat16):
    return jnp.clip(width * jax.random.normal(key, shape, jnp.float32), -bound, bound).astype(dtype)


def setup_inputs(seed: int = 0) -> dict:
    key_of = jax.random.split(jax.random.key(seed), 12)
    image = draw_image(jax.random.fold_in(key_of[11], 71), 0)
    bn_gain = jnp.clip(jnp.exp(jax.random.uniform(key_of[1], (CHANNELS,), jnp.float32, math.log(0.5), math.log(2.0))), 0.5, 2.0)
    bn_shift = gaussian(key_of[2], (CHANNELS,), 0.5, 3.0, jnp.float32)
    expand_weight = gaussian(key_of[3], (CHANNELS, HIDDEN_CH), CHANNELS ** -0.5, 0.375)
    expand_bias = gaussian(key_of[4], (HIDDEN_CH,), 0.5, 3.0, jnp.float32)
    depth_kernel = gaussian(key_of[5], (3, 3, HIDDEN_CH), 9 ** -0.5, 2.0)
    depth_bias = gaussian(key_of[6], (HIDDEN_CH,), 0.5, 3.0, jnp.float32)
    project_weight = gaussian(key_of[7], (HIDDEN_CH, CHANNELS), HIDDEN_CH ** -0.5, 0.1875)
    norm_gain = jnp.clip(jnp.exp(jax.random.uniform(key_of[8], (2, CHANNELS), jnp.float32, math.log(0.5), math.log(2.0))), 0.5, 2.0)
    qkv_weight = draw_qkv_weight(jax.random.fold_in(key_of[11], 71), 0)
    out_weight = gaussian(key_of[10], (2, CHANNELS, CHANNELS), CHANNELS ** -0.5, 0.375)
    return dict(image=image, bn_gain=bn_gain, bn_shift=bn_shift, expand_weight=expand_weight, expand_bias=expand_bias, depth_kernel=depth_kernel, depth_bias=depth_bias, project_weight=project_weight, norm_gain=norm_gain, qkv_weight=qkv_weight, out_weight=out_weight)


def layer_norm(values, gain):
    mean = lax.optimization_barrier(jnp.mean(values, axis=-1, keepdims=True))
    centred = values - mean
    spread = lax.optimization_barrier(jnp.mean(centred * centred, axis=-1, keepdims=True))
    return centred * lax.rsqrt(spread + 1e-05) * gain

def attend(tokens, gain, qkv_weight, out_weight):
    groups, length, chans = tokens.shape
    values = tokens.astype(jnp.float32)
    normed = layer_norm(values, gain).astype(jnp.bfloat16)
    proj = jnp.dot(normed.reshape(groups * length, chans), qkv_weight, preferred_element_type=jnp.float32).astype(jnp.bfloat16)
    proj = proj.reshape(groups, length, 3, HEADS, chans // HEADS)
    query = proj[:, :, 0].astype(jnp.float32)
    keys = proj[:, :, 1].astype(jnp.float32)
    vals = proj[:, :, 2].astype(jnp.float32)
    scores = jnp.einsum('gqhd,gkhd->ghqk', query, keys) * (chans // HEADS) ** (-0.5)
    top = lax.optimization_barrier(jnp.max(scores, axis=-1, keepdims=True))
    weights = jnp.exp(scores - top)
    probs = (weights / lax.optimization_barrier(jnp.sum(weights, axis=-1, keepdims=True))).astype(jnp.bfloat16)
    mixed = jnp.einsum('ghqk,gkhd->gqhd', probs.astype(jnp.float32), vals).astype(jnp.bfloat16)
    moved = jnp.dot(mixed.reshape(groups * length, chans), out_weight, preferred_element_type=jnp.float32)
    return (values + moved.reshape(groups, length, chans)).astype(jnp.bfloat16)

def reference(image, bn_gain, bn_shift, expand_weight, expand_bias, depth_kernel, depth_bias, project_weight, norm_gain, qkv_weight, out_weight):
    rows, cols, chans = image.shape
    wide = expand_weight.shape[1]
    strip = 16
    padded = jnp.pad(image, ((1, 1), (0, 0), (0, 0)))
    kernel = depth_kernel.astype(jnp.float32)

    def one_strip(index):
        start = index.astype(jnp.int32) * strip
        piece = lax.dynamic_slice_in_dim(padded, start, strip + 2, 0)
        normed = (piece.astype(jnp.float32) * bn_gain + bn_shift).astype(jnp.bfloat16)
        hidden = jnp.dot(normed.reshape(-1, chans), expand_weight, preferred_element_type=jnp.float32) + expand_bias
        hidden = jax.nn.gelu(hidden).astype(jnp.bfloat16).reshape(strip + 2, cols, wide)
        row_ids = start - 1 + jnp.arange(strip + 2).astype(jnp.int32)
        keep = (row_ids >= 0) & (row_ids < rows)
        hidden = jnp.where(keep[:, None, None], hidden, jnp.zeros_like(hidden))
        hidden = jnp.pad(hidden, ((0, 0), (1, 1), (0, 0)))
        total = jnp.zeros((strip, cols, wide), jnp.float32)
        for down in range(3):
            for across in range(3):
                total = total + hidden[down:down + strip, across:across + cols].astype(jnp.float32) * kernel[down, across]
        middle = jax.nn.gelu(total + depth_bias).astype(jnp.bfloat16)
        moved = jnp.dot(middle.reshape(-1, wide), project_weight, preferred_element_type=jnp.float32)
        return (piece[1:strip + 1].astype(jnp.float32) + moved.reshape(strip, cols, chans)).astype(jnp.bfloat16)
    after_conv = lax.map(one_strip, jnp.arange(rows // strip)).reshape(rows, cols, chans)
    wins = after_conv.reshape(rows // WINDOW, WINDOW, cols // WINDOW, WINDOW, chans).transpose(0, 2, 1, 3, 4)
    wins = wins.reshape(rows // WINDOW, cols // WINDOW, WINDOW * WINDOW, chans)

    def block_row(group):
        return attend(group, norm_gain[0], qkv_weight[0], out_weight[0])
    done = lax.map(block_row, wins)
    after_block = done.reshape(rows // WINDOW, cols // WINDOW, WINDOW, WINDOW, chans).transpose(0, 2, 1, 3, 4).reshape(rows, cols, chans)
    stride_row = rows // GRID_SIDE
    stride_col = cols // GRID_SIDE
    sets = after_block.reshape(GRID_SIDE, stride_row, GRID_SIDE, stride_col, chans).transpose(1, 3, 0, 2, 4)
    sets = sets.reshape(stride_row, stride_col, GRID_SIDE * GRID_SIDE, chans)

    def grid_row(group):
        return attend(group, norm_gain[1], qkv_weight[1], out_weight[1])
    finished = lax.map(grid_row, sets)
    finished = finished.reshape(stride_row, stride_col, GRID_SIDE, GRID_SIDE, chans).transpose(2, 0, 3, 1, 4)
    return finished.reshape(rows, cols, chans)
```

```python
import math

import jax
import jax.numpy as jnp
from jax import lax
from jax.experimental import pallas as pl
from jax.experimental.pallas import tpu as pltpu
from jax.sharding import PartitionSpec as P

HEADS = 8
WINDOW = 8
GRID_SIDE = 16


def padded(cells, sides, width):
    for axis, dim in sides:
        count = lax.axis_size(axis)
        ends = count - 1
        head = lax.slice_in_dim(cells, 0, width, axis=dim)
        tail = lax.slice_in_dim(cells, cells.shape[dim] - width, cells.shape[dim], axis=dim)
        cells = jnp.concatenate(
            [
                lax.ppermute(tail, axis, [(i, (i + 1) % count) for i in range(ends)]),
                cells,
                lax.ppermute(head, axis, [((i + 1) % count, i) for i in range(ends)]),
            ],
            axis=dim,
        )
    return cells


def layer_norm(values, gain):
    mean = jnp.mean(values, axis=-1, keepdims=True)
    centred = values - mean
    spread = jnp.mean(centred * centred, axis=-1, keepdims=True)
    return centred * lax.rsqrt(spread + 1e-05) * gain


def expand_pixels(pixels, bn_gain, bn_shift, expand_weight, expand_bias):
    shape = pixels.shape
    normed = (pixels.astype(jnp.float32) * bn_gain + bn_shift).astype(jnp.bfloat16)
    hidden = (
        jnp.dot(normed.reshape(-1, shape[-1]), expand_weight, preferred_element_type=jnp.float32)
        + expand_bias
    )
    return jax.nn.gelu(hidden).astype(jnp.bfloat16).reshape(shape[:-1] + (expand_weight.shape[1],))


def depth_project(framed, residual, depth_kernel, depth_bias, project_weight):
    height = residual.shape[0]
    width = residual.shape[1]
    kernel = depth_kernel.astype(jnp.float32)
    total = jnp.zeros((height, width, framed.shape[2]), jnp.float32)
    for down in range(3):
        for across in range(3):
            total = (
                total
                + framed[down : down + height, across : across + width].astype(jnp.float32)
                * kernel[down, across]
            )
    middle = jax.nn.gelu(total + depth_bias).astype(jnp.bfloat16)
    moved = jnp.dot(
        middle.reshape(height * width, -1), project_weight, preferred_element_type=jnp.float32
    )
    return (residual.astype(jnp.float32) + moved.reshape(height, width, -1)).astype(jnp.bfloat16)


def attend(tokens, gain, qkv_weight, out_weight):
    groups, length, chans = tokens.shape
    values = tokens.astype(jnp.float32)
    normed = layer_norm(values, gain).astype(jnp.bfloat16)
    proj = jnp.dot(
        normed.reshape(groups * length, chans), qkv_weight, preferred_element_type=jnp.float32
    ).astype(jnp.bfloat16)
    proj = proj.reshape(groups, length, 3, HEADS, chans // HEADS)
    query = proj[:, :, 0]
    keys = proj[:, :, 1]
    vals = proj[:, :, 2]
    scores = jnp.einsum("gqhd,gkhd->ghqk", query, keys, preferred_element_type=jnp.float32) * (
        chans // HEADS
    ) ** (-0.5)
    top = jnp.max(scores, axis=-1, keepdims=True)
    weights = jnp.exp(scores - top)
    probs = (weights / jnp.sum(weights, axis=-1, keepdims=True)).astype(jnp.bfloat16)
    mixed = jnp.einsum("ghqk,gkhd->gqhd", probs, vals, preferred_element_type=jnp.float32).astype(
        jnp.bfloat16
    )
    moved = jnp.dot(
        mixed.reshape(groups * length, chans), out_weight, preferred_element_type=jnp.float32
    )
    return (values + moved.reshape(groups, length, chans)).astype(jnp.bfloat16)


def attend_batched(tokens, gain, qkv_weight, out_weight, wanted):
    groups = tokens.shape[0]
    per_step = math.gcd(groups, wanted)
    stacked = tokens.reshape((groups // per_step, per_step) + tokens.shape[1:])

    def one_batch(batch):
        return attend(batch, gain, qkv_weight, out_weight)

    return lax.map(one_batch, stacked).reshape(tokens.shape)


def per_device(
    image,
    bn_gain,
    bn_shift,
    expand_weight,
    expand_bias,
    depth_kernel,
    depth_bias,
    project_weight,
    norm_gain,
    qkv_weight,
    out_weight,
):
    rows_dev, cols_dev, chans = image.shape
    row_count = lax.axis_size("row")
    col_count = lax.axis_size("col")
    strips = rows_dev // WINDOW

    def expand_strip(index):
        piece = lax.dynamic_slice_in_dim(image, index * WINDOW, WINDOW, 0)
        return expand_pixels(piece, bn_gain, bn_shift, expand_weight, expand_bias)

    hidden = lax.map(expand_strip, jnp.arange(strips)).reshape(rows_dev, cols_dev, -1)
    framed_all = padded(hidden, (("row", 0), ("col", 1)), 1)

    def mix_strip(index):
        framed = lax.dynamic_slice_in_dim(framed_all, index * WINDOW, WINDOW + 2, 0)
        residual = lax.dynamic_slice_in_dim(image, index * WINDOW, WINDOW, 0)
        return depth_project(framed, residual, depth_kernel, depth_bias, project_weight)

    after_conv = lax.map(mix_strip, jnp.arange(strips)).reshape(rows_dev, cols_dev, chans)
    windows = after_conv.reshape(
        rows_dev // WINDOW, WINDOW, cols_dev // WINDOW, WINDOW, chans
    ).transpose(0, 2, 1, 3, 4)
    windows = windows.reshape(-1, WINDOW * WINDOW, chans)
    windows = attend_batched(windows, norm_gain[0], qkv_weight[0], out_weight[0], 16)
    after_block = windows.reshape(
        rows_dev // WINDOW, cols_dev // WINDOW, WINDOW, WINDOW, chans
    ).transpose(0, 2, 1, 3, 4)
    after_block = after_block.reshape(rows_dev, cols_dev, chans)
    rep_row = GRID_SIDE // row_count
    rep_col = GRID_SIDE // col_count
    low_row = rows_dev // GRID_SIDE
    low_col = cols_dev // GRID_SIDE
    items = low_row * low_col
    local = rep_row * rep_col
    devices = row_count * col_count
    arranged = after_block.reshape(
        rep_row, row_count, low_row, rep_col, col_count, low_col, chans
    ).transpose(1, 4, 2, 5, 0, 3, 6)
    outgoing = arranged.reshape(devices, 1, items, local, chans)
    received = lax.all_to_all(outgoing, ("row", "col"), split_axis=0, concat_axis=1, tiled=True)
    count = received.shape[2]
    tokens = (
        received.reshape(devices, count, local, chans)
        .transpose(1, 0, 2, 3)
        .reshape(count, devices * local, chans)
    )
    done = attend_batched(tokens, norm_gain[1], qkv_weight[1], out_weight[1], 2)
    reply = (
        done.reshape(count, devices, local, chans)
        .transpose(1, 0, 2, 3)
        .reshape(1, devices, count, local, chans)
    )
    returned = lax.all_to_all(reply, ("row", "col"), split_axis=1, concat_axis=0, tiled=True)
    placed = returned.reshape(
        row_count, col_count, low_row, low_col, rep_row, rep_col, chans
    ).transpose(4, 0, 2, 5, 1, 3, 6)
    return placed.reshape(rows_dev, cols_dev, chans)


NT = (((1,), (1,)), ((), ()))
TN = (((0,), (0,)), ((), ()))
F32 = jnp.float32
BF16 = jnp.bfloat16
GELU_IN = math.sqrt(2.0 / math.pi)


def dot(a, b, dims=(((1,), (0,)), ((), ()))):
    return lax.dot_general(a, b, dims, preferred_element_type=F32)


def gelu_bf16(x):
    x = x.astype(BF16)
    inner = x * (x * x * BF16(GELU_IN * 0.044715) + BF16(GELU_IN))
    half = x * BF16(0.5)
    return half + half * jnp.tanh(inner)


def norm_rows(x, gain):
    mean = jnp.mean(x, axis=-1, keepdims=True)
    centred = x - mean
    spread = jnp.mean(centred * centred, axis=-1, keepdims=True)
    return (centred * lax.rsqrt(spread + 1e-05) * gain).astype(BF16)


def head_rows(q_t, head, size):
    chans, width = q_t.shape
    parts = []
    if head:
        parts.append(jnp.zeros((head * size, width), BF16))
    parts.append(q_t[head * size : (head + 1) * size])
    if (head + 1) * size < chans:
        parts.append(jnp.zeros((chans - (head + 1) * size, width), BF16))
    return jnp.concatenate(parts, axis=0)


def project_qkv(x, gain, wq_t, wk, wv_t, size):
    ln = norm_rows(x, gain)
    scale = math.log2(math.e) / math.sqrt(size)
    q_t = (dot(wq_t, ln, NT) * scale).astype(BF16)
    k = dot(ln, wk).astype(BF16)
    v_t = dot(wv_t, ln, NT).astype(BF16)
    return q_t, k, v_t


def window_attend(x, gain, wq_t, wk, wv_t, wo):
    tokens, chans = x.shape
    size = chans // HEADS
    q_t, k, v_t = project_qkv(x, gain, wq_t, wk, wv_t, size)
    lane = lax.broadcasted_iota(jnp.int32, (64, 256), 1)
    low = (lane % 128) < 64
    low_mask = low.astype(F32).astype(BF16)
    high_mask = (1.0 - low.astype(F32)).astype(BF16)
    ones = jnp.ones((16, 128), BF16)
    columns = []
    for pair in range(tokens // 128):
        at = slice(pair * 128, pair * 128 + 128)
        k_p = k[at]
        mixed = []
        for h in range(0, HEADS, 2):
            rhs = jnp.concatenate(
                [head_rows(q_t[:, at], h, size), head_rows(q_t[:, at], h + 1, size)], axis=1
            )
            s = dot(k_p, rhs)
            s = jnp.where(low, s[:64], s[64:])
            p = jnp.exp2(s - jnp.max(s, axis=0, keepdims=True)).astype(BF16)
            p = jnp.concatenate([p * low_mask, p * high_mask], axis=0)
            lhs = jnp.concatenate([v_t[h * size : (h + 2) * size, at], ones], axis=0)
            o = dot(lhs, p)
            inv = 1.0 / o[2 * size : 2 * size + 1]
            mixed.append((o[:size, :128] * inv[:, :128]).astype(BF16))
            mixed.append((o[size : 2 * size, 128:] * inv[:, 128:]).astype(BF16))
        columns.append(jnp.concatenate(mixed, axis=0))
    mixed_t = jnp.concatenate(columns, axis=1)
    return x + dot(mixed_t, wo, TN)


def set_attend(x, gain, wq_t, wk, wv_t, wo):
    tokens, chans = x.shape
    size = chans // HEADS
    q_t, k, v_t = project_qkv(x, gain, wq_t, wk, wv_t, size)
    ones = jnp.ones((16, tokens), BF16)
    mixed = []
    for h in range(HEADS):
        s = dot(k, head_rows(q_t, h, size))
        p = jnp.exp2(s - jnp.max(s, axis=0, keepdims=True)).astype(BF16)
        lhs = jnp.concatenate([v_t[h * size : (h + 1) * size], ones], axis=0)
        o = dot(lhs, p)
        mixed.append((o[:size] * (1.0 / o[size : size + 1])).astype(BF16))
    return x + dot(jnp.concatenate(mixed, axis=0), wo, TN)


def put_halves(ref, rows, value):
    ref[0, rows, :] = value[:, :128]
    ref[1, rows, :] = value[:, 128:]


def strided(ref, start, count, stride):
    rows = pl.ds(start, count, stride=stride)
    return jnp.concatenate([ref[0, rows, :], ref[1, rows, :]], axis=1)


def hidden_row(
    row, img, left, right, bn_gain, bn_shift, expand_w, expand_b, edge_low, edge_high, rowbuf, hid
):
    gain = bn_gain[...]
    shift = bn_shift[...]
    put_halves(rowbuf, slice(8, 136), img[row].astype(F32) * gain + shift)
    put_halves(rowbuf, slice(7, 8), left[pl.ds(row, 1), :] * gain + shift)
    put_halves(rowbuf, slice(136, 137), right[pl.ds(row, 1), :] * gain + shift)
    planes = [strided(rowbuf, 7 + j, 16, 8) for j in range(10)]
    normed = jnp.concatenate(planes, axis=0).astype(BF16)
    for c in range(0, expand_w.shape[1], 256):
        h = dot(normed, expand_w[:, c : c + 256]) + expand_b[:, c : c + 256]
        h = gelu_bf16(h).reshape(10, 16, 256)
        hid[row, :, :, c : c + 256] = h
        hid[row, 0, :, c : c + 256] = h[0] * edge_low
        hid[row, 9, :, c : c + 256] = h[9] * edge_high


def mix_row(strip, r, slot, img, depth_k, depth_b, project_w, hid, mid, moved, conv):
    row = strip * WINDOW + r
    for c in range(0, hid.shape[3], 256):
        at = slice(c, c + 256)
        for j0 in range(0, 8, 4):
            total = None
            for u in range(3):
                part = None
                for v in range(3):
                    term = hid[row + u, j0 + v : j0 + v + 4, :, at] * depth_k[u * 3 + v : u * 3 + v + 1, at][None]
                    part = term if part is None else part + term
                part = part.astype(F32)
                total = part if total is None else total + part
            total = total + depth_b[:, at][None]
            mid[j0 * 16 : j0 * 16 + 64, at] = gelu_bf16(total).reshape(64, 256)
    put_halves(moved, slice(0, 128), dot(mid[...], project_w[...]))
    base = img[row + 1].astype(F32)
    for s in range(16):
        value = strided(moved, s, 8, 16) + base[s * 8 : s * 8 + 8]
        conv[slot, s, pl.ds(pl.multiple_of(r * 8, 8), 8), :] = value


def front_kernel(
    img, left, right, masks, bn_gain, bn_shift, expand_w, expand_b, depth_k, depth_b, project_w,
    gain, wq_t, wk, wv_t, wo, send, rowbuf, hid, mid, moved, conv, obuf,
):
    edge_low = masks[0]
    edge_high = masks[1]

    def hide(row, _):
        hidden_row(
            row, img, left, right, bn_gain, bn_shift, expand_w, expand_b, edge_low, edge_high,
            rowbuf, hid,
        )
        return 0

    lax.fori_loop(0, 34, hide, 0)
    for c in range(0, hid.shape[3], 256):
        hid[0, :, :, c : c + 256] = hid[0, :, :, c : c + 256] * masks[2][None]
        hid[33, :, :, c : c + 256] = hid[33, :, :, c : c + 256] * masks[3][None]
    for half in range(2):
        for p in range(2):

            def mix(r, _):
                mix_row(p * 2 + half, r, p, img, depth_k, depth_b, project_w, hid, mid, moved, conv)
                return 0

            lax.fori_loop(0, 8, mix, 0)

        def attend_chunk(m, _):
            x = jnp.concatenate([conv[w // 4, (w % 4) * 4 + m] for w in range(8)], axis=0)
            value = window_attend(x, gain[...], wq_t[...], wk[...], wv_t[...], wo[...])
            put_halves(obuf, slice(0, 512), value)
            for d in range(32):
                block = [strided(obuf, 2 * d + e, 8, 64) for e in range(2)]
                send[d, half * 4 + m] = jnp.concatenate(block, axis=0).astype(BF16)
            return 0

        lax.fori_loop(0, 4, attend_chunk, 0)


def back_kernel(received, gain, wq_t, wk, wv_t, wo, reply):
    def one(c, _):
        blocks = received[:, c].astype(F32)
        done = [
            set_attend(
                blocks[:, e * 8 : e * 8 + 8].reshape(256, 256), gain[...], wq_t[...], wk[...], wv_t[...], wo[...]
            ).reshape(32, 8, 256)
            for e in range(2)
        ]
        reply[:, c] = jnp.concatenate(done, axis=1).astype(BF16)
        return 0

    lax.fori_loop(0, received.shape[1], one, 0)


def shift_pair(first, last, axis):
    count = lax.axis_size(axis)
    ends = count - 1
    before = lax.ppermute(last, axis, [(i, i + 1) for i in range(ends)])
    after = lax.ppermute(first, axis, [(i + 1, i) for i in range(ends)])
    return before, after


def halo(image):
    top, bottom = shift_pair(image[:1], image[-1:], "row")
    img = jnp.concatenate([top, image, bottom], axis=0)
    left, right = shift_pair(img[:, 0], img[:, -1], "col")
    return img, left.astype(F32), right.astype(F32)


def edge_masks():
    row = lax.axis_index("row")
    col = lax.axis_index("col")
    s = jnp.arange(16)[:, None]
    low = jnp.where((col == 0) & (s == 0), 0.0, 1.0)
    high = jnp.where((col == lax.axis_size("col") - 1) & (s == 15), 0.0, 1.0)
    top = jnp.where(row == 0, 0.0, 1.0) * jnp.ones((16, 1))
    bottom = jnp.where(row == lax.axis_size("row") - 1, 0.0, 1.0) * jnp.ones((16, 1))
    masks = jnp.stack([low, high, top, bottom]).astype(BF16)
    return jnp.broadcast_to(masks, (4, 16, 256))


def split_weights(norm_gain, qkv_weight, out_weight, s):
    chans = qkv_weight.shape[1]
    w = qkv_weight[s]
    return (
        norm_gain[s][None],
        w[:, :chans].T,
        w[:, chans : 2 * chans],
        w[:, 2 * chans :].T,
        out_weight[s],
    )


VMEM = pl.BlockSpec(memory_space=pltpu.VMEM)


def per_device_fast(
    image, bn_gain, bn_shift, expand_weight, expand_bias, depth_kernel, depth_bias, project_weight,
    norm_gain, qkv_weight, out_weight,
):
    wide = expand_weight.shape[1]
    img, left, right = halo(image)
    masks = edge_masks()
    send = pl.pallas_call(
        front_kernel,
        out_shape=jax.ShapeDtypeStruct((32, 8, 16, 256), BF16),
        in_specs=[VMEM] * 16,
        out_specs=VMEM,
        scratch_shapes=[
            pltpu.VMEM((2, 144, 128), F32),
            pltpu.VMEM((34, 10, 16, wide), BF16),
            pltpu.VMEM((128, wide), BF16),
            pltpu.VMEM((2, 128, 128), F32),
            pltpu.VMEM((2, 16, 64, 256), F32),
            pltpu.VMEM((2, 512, 128), F32),
        ],
        compiler_params=pltpu.CompilerParams(vmem_limit_bytes=56 * 1024 * 1024),
    )(
        img, left, right, masks, bn_gain[None], bn_shift[None], expand_weight, expand_bias[None],
        depth_kernel.reshape(9, wide), depth_bias[None], project_weight,
        *split_weights(norm_gain, qkv_weight, out_weight, 0),
    )
    received = lax.all_to_all(send, ("row", "col"), split_axis=0, concat_axis=0, tiled=True)
    reply = pl.pallas_call(
        back_kernel,
        out_shape=jax.ShapeDtypeStruct((32, 8, 16, 256), BF16),
        in_specs=[VMEM] * 6,
        out_specs=VMEM,
        compiler_params=pltpu.CompilerParams(vmem_limit_bytes=56 * 1024 * 1024),
    )(received, *split_weights(norm_gain, qkv_weight, out_weight, 1))
    returned = lax.all_to_all(reply, ("row", "col"), split_axis=0, concat_axis=0, tiled=True)
    placed = returned.reshape(8, 4, 2, 4, 2, 2, 4, 256).transpose(5, 2, 0, 6, 3, 1, 4, 7)
    return placed.reshape(image.shape)


def solution(mesh):
    in_specs = (P("row", "col", None), P(), P(), P(), P(), P(), P(), P(), P(), P(), P())
    out_specs = P("row", "col", None)
    fast = mesh.shape["row"] == 8 and mesh.shape["col"] == 4
    return jax.shard_map(
        per_device_fast if fast else per_device, mesh=mesh, in_specs=in_specs, out_specs=out_specs, check_vma=False
    )
```

```python
import math

import jax
import jax.numpy as jnp
from jax import lax
from jax.experimental import pallas as pl
from jax.experimental.pallas import tpu as pltpu
from jax.sharding import PartitionSpec as P

HEADS = 8
WINDOW = 8
GRID_SIDE = 16


def padded(cells, sides, width):
    for axis, dim in sides:
        count = lax.axis_size(axis)
        ends = count - 1
        head = lax.slice_in_dim(cells, 0, width, axis=dim)
        tail = lax.slice_in_dim(cells, cells.shape[dim] - width, cells.shape[dim], axis=dim)
        cells = jnp.concatenate(
            [
                lax.ppermute(tail, axis, [(i, (i + 1) % count) for i in range(ends)]),
                cells,
                lax.ppermute(head, axis, [((i + 1) % count, i) for i in range(ends)]),
            ],
            axis=dim,
        )
    return cells


def layer_norm(values, gain):
    mean = jnp.mean(values, axis=-1, keepdims=True)
    centred = values - mean
    spread = jnp.mean(centred * centred, axis=-1, keepdims=True)
    return centred * lax.rsqrt(spread + 1e-05) * gain


def expand_pixels(pixels, bn_gain, bn_shift, expand_weight, expand_bias):
    shape = pixels.shape
    normed = (pixels.astype(jnp.float32) * bn_gain + bn_shift).astype(jnp.bfloat16)
    hidden = (
        jnp.dot(normed.reshape(-1, shape[-1]), expand_weight, preferred_element_type=jnp.float32)
        + expand_bias
    )
    return jax.nn.gelu(hidden).astype(jnp.bfloat16).reshape(shape[:-1] + (expand_weight.shape[1],))


def depth_project(framed, residual, depth_kernel, depth_bias, project_weight):
    height = residual.shape[0]
    width = residual.shape[1]
    kernel = depth_kernel.astype(jnp.float32)
    total = jnp.zeros((height, width, framed.shape[2]), jnp.float32)
    for down in range(3):
        for across in range(3):
            total = (
                total
                + framed[down : down + height, across : across + width].astype(jnp.float32)
                * kernel[down, across]
            )
    middle = jax.nn.gelu(total + depth_bias).astype(jnp.bfloat16)
    moved = jnp.dot(
        middle.reshape(height * width, -1), project_weight, preferred_element_type=jnp.float32
    )
    return (residual.astype(jnp.float32) + moved.reshape(height, width, -1)).astype(jnp.bfloat16)


def attend(tokens, gain, qkv_weight, out_weight):
    groups, length, chans = tokens.shape
    values = tokens.astype(jnp.float32)
    normed = layer_norm(values, gain).astype(jnp.bfloat16)
    proj = jnp.dot(
        normed.reshape(groups * length, chans), qkv_weight, preferred_element_type=jnp.float32
    ).astype(jnp.bfloat16)
    proj = proj.reshape(groups, length, 3, HEADS, chans // HEADS)
    query = proj[:, :, 0]
    keys = proj[:, :, 1]
    vals = proj[:, :, 2]
    scores = jnp.einsum("gqhd,gkhd->ghqk", query, keys, preferred_element_type=jnp.float32) * (
        chans // HEADS
    ) ** (-0.5)
    top = jnp.max(scores, axis=-1, keepdims=True)
    weights = jnp.exp(scores - top)
    probs = (weights / jnp.sum(weights, axis=-1, keepdims=True)).astype(jnp.bfloat16)
    mixed = jnp.einsum("ghqk,gkhd->gqhd", probs, vals, preferred_element_type=jnp.float32).astype(
        jnp.bfloat16
    )
    moved = jnp.dot(
        mixed.reshape(groups * length, chans), out_weight, preferred_element_type=jnp.float32
    )
    return (values + moved.reshape(groups, length, chans)).astype(jnp.bfloat16)


def attend_batched(tokens, gain, qkv_weight, out_weight, wanted):
    groups = tokens.shape[0]
    per_step = math.gcd(groups, wanted)
    stacked = tokens.reshape((groups // per_step, per_step) + tokens.shape[1:])

    def one_batch(batch):
        return attend(batch, gain, qkv_weight, out_weight)

    return lax.map(one_batch, stacked).reshape(tokens.shape)


def per_device(
    image,
    bn_gain,
    bn_shift,
    expand_weight,
    expand_bias,
    depth_kernel,
    depth_bias,
    project_weight,
    norm_gain,
    qkv_weight,
    out_weight,
):
    rows_dev, cols_dev, chans = image.shape
    row_count = lax.axis_size("row")
    col_count = lax.axis_size("col")
    strips = rows_dev // WINDOW

    def expand_strip(index):
        piece = lax.dynamic_slice_in_dim(image, index * WINDOW, WINDOW, 0)
        return expand_pixels(piece, bn_gain, bn_shift, expand_weight, expand_bias)

    hidden = lax.map(expand_strip, jnp.arange(strips)).reshape(rows_dev, cols_dev, -1)
    framed_all = padded(hidden, (("row", 0), ("col", 1)), 1)

    def mix_strip(index):
        framed = lax.dynamic_slice_in_dim(framed_all, index * WINDOW, WINDOW + 2, 0)
        residual = lax.dynamic_slice_in_dim(image, index * WINDOW, WINDOW, 0)
        return depth_project(framed, residual, depth_kernel, depth_bias, project_weight)

    after_conv = lax.map(mix_strip, jnp.arange(strips)).reshape(rows_dev, cols_dev, chans)
    windows = after_conv.reshape(
        rows_dev // WINDOW, WINDOW, cols_dev // WINDOW, WINDOW, chans
    ).transpose(0, 2, 1, 3, 4)
    windows = windows.reshape(-1, WINDOW * WINDOW, chans)
    windows = attend_batched(windows, norm_gain[0], qkv_weight[0], out_weight[0], 16)
    after_block = windows.reshape(
        rows_dev // WINDOW, cols_dev // WINDOW, WINDOW, WINDOW, chans
    ).transpose(0, 2, 1, 3, 4)
    after_block = after_block.reshape(rows_dev, cols_dev, chans)
    rep_row = GRID_SIDE // row_count
    rep_col = GRID_SIDE // col_count
    low_row = rows_dev // GRID_SIDE
    low_col = cols_dev // GRID_SIDE
    items = low_row * low_col
    local = rep_row * rep_col
    devices = row_count * col_count
    arranged = after_block.reshape(
        rep_row, row_count, low_row, rep_col, col_count, low_col, chans
    ).transpose(1, 4, 2, 5, 0, 3, 6)
    outgoing = arranged.reshape(devices, 1, items, local, chans)
    received = lax.all_to_all(outgoing, ("row", "col"), split_axis=0, concat_axis=1, tiled=True)
    count = received.shape[2]
    tokens = (
        received.reshape(devices, count, local, chans)
        .transpose(1, 0, 2, 3)
        .reshape(count, devices * local, chans)
    )
    done = attend_batched(tokens, norm_gain[1], qkv_weight[1], out_weight[1], 2)
    reply = (
        done.reshape(count, devices, local, chans)
        .transpose(1, 0, 2, 3)
        .reshape(1, devices, count, local, chans)
    )
    returned = lax.all_to_all(reply, ("row", "col"), split_axis=1, concat_axis=0, tiled=True)
    placed = returned.reshape(
        row_count, col_count, low_row, low_col, rep_row, rep_col, chans
    ).transpose(4, 0, 2, 5, 1, 3, 6)
    return placed.reshape(rows_dev, cols_dev, chans)


NT = (((1,), (1,)), ((), ()))
TN = (((0,), (0,)), ((), ()))
F32 = jnp.float32
BF16 = jnp.bfloat16
GELU_IN = math.sqrt(2.0 / math.pi)


def dot(a, b, dims=(((1,), (0,)), ((), ()))):
    return lax.dot_general(a, b, dims, preferred_element_type=F32)


def gelu_bf16(x):
    x = x.astype(BF16)
    inner = x * (x * x * BF16(GELU_IN * 0.044715) + BF16(GELU_IN))
    half = x * BF16(0.5)
    return half + half * jnp.tanh(inner)


def norm_rows(x, gain):
    mean = jnp.mean(x, axis=-1, keepdims=True)
    centred = x - mean
    spread = jnp.mean(centred * centred, axis=-1, keepdims=True)
    return (centred * lax.rsqrt(spread + 1e-05) * gain).astype(BF16)


def head_rows(q_t, head, size):
    chans, width = q_t.shape
    parts = []
    if head:
        parts.append(jnp.zeros((head * size, width), BF16))
    parts.append(q_t[head * size : (head + 1) * size])
    if (head + 1) * size < chans:
        parts.append(jnp.zeros((chans - (head + 1) * size, width), BF16))
    return jnp.concatenate(parts, axis=0)


def project_qkv(x, gain, wq_t, wk, wv_t, size):
    ln = norm_rows(x, gain)
    scale = math.log2(math.e) / math.sqrt(size)
    q_t = (dot(wq_t, ln, NT) * scale).astype(BF16)
    k = dot(ln, wk).astype(BF16)
    v_t = dot(wv_t, ln, NT).astype(BF16)
    return q_t, k, v_t


def window_attend(x, gain, wq_t, wk, wv_t, wo):
    tokens, chans = x.shape
    size = chans // HEADS
    q_t, k, v_t = project_qkv(x, gain, wq_t, wk, wv_t, size)
    lane = lax.broadcasted_iota(jnp.int32, (64, 256), 1)
    low = (lane % 128) < 64
    low_mask = low.astype(F32).astype(BF16)
    high_mask = (1.0 - low.astype(F32)).astype(BF16)
    ones = jnp.ones((16, 128), BF16)
    columns = []
    for pair in range(tokens // 128):
        at = slice(pair * 128, pair * 128 + 128)
        k_p = k[at]
        mixed = []
        for h in range(0, HEADS, 2):
            rhs = jnp.concatenate(
                [head_rows(q_t[:, at], h, size), head_rows(q_t[:, at], h + 1, size)], axis=1
            )
            s = dot(k_p, rhs)
            s = jnp.where(low, s[:64], s[64:])
            p = jnp.exp2(s - jnp.max(s, axis=0, keepdims=True)).astype(BF16)
            p = jnp.concatenate([p * low_mask, p * high_mask], axis=0)
            lhs = jnp.concatenate([v_t[h * size : (h + 2) * size, at], ones], axis=0)
            o = dot(lhs, p)
            inv = 1.0 / o[2 * size : 2 * size + 1]
            mixed.append((o[:size, :128] * inv[:, :128]).astype(BF16))
            mixed.append((o[size : 2 * size, 128:] * inv[:, 128:]).astype(BF16))
        columns.append(jnp.concatenate(mixed, axis=0))
    mixed_t = jnp.concatenate(columns, axis=1)
    return x + dot(mixed_t, wo, TN)


def set_attend(x, gain, wq_t, wk, wv_t, wo):
    tokens, chans = x.shape
    size = chans // HEADS
    q_t, k, v_t = project_qkv(x, gain, wq_t, wk, wv_t, size)
    ones = jnp.ones((16, tokens), BF16)
    mixed = []
    for h in range(HEADS):
        s = dot(k, head_rows(q_t, h, size))
        p = jnp.exp2(s - jnp.max(s, axis=0, keepdims=True)).astype(BF16)
        lhs = jnp.concatenate([v_t[h * size : (h + 1) * size], ones], axis=0)
        o = dot(lhs, p)
        mixed.append((o[:size] * (1.0 / o[size : size + 1])).astype(BF16))
    return x + dot(jnp.concatenate(mixed, axis=0), wo, TN)


def put_halves(ref, rows, value):
    ref[0, rows, :] = value[:, :128]
    ref[1, rows, :] = value[:, 128:]


def strided(ref, start, count, stride):
    rows = pl.ds(start, count, stride=stride)
    return jnp.concatenate([ref[0, rows, :], ref[1, rows, :]], axis=1)


def hidden_row(
    row, img, left, right, bn_gain, bn_shift, expand_w, expand_b, edge_low, edge_high, rowbuf, hid
):
    gain = bn_gain[...]
    shift = bn_shift[...]
    put_halves(rowbuf, slice(8, 136), img[row].astype(F32) * gain + shift)
    put_halves(rowbuf, slice(7, 8), left[pl.ds(row, 1), :] * gain + shift)
    put_halves(rowbuf, slice(136, 137), right[pl.ds(row, 1), :] * gain + shift)
    planes = [strided(rowbuf, 7 + j, 16, 8) for j in range(10)]
    normed = jnp.concatenate(planes, axis=0).astype(BF16)
    for c in range(0, expand_w.shape[1], 256):
        h = dot(normed, expand_w[:, c : c + 256]) + expand_b[:, c : c + 256]
        h = gelu_bf16(h).reshape(10, 16, 256)
        hid[row, :, :, c : c + 256] = h
        hid[row, 0, :, c : c + 256] = h[0] * edge_low
        hid[row, 9, :, c : c + 256] = h[9] * edge_high


def mix_row(strip, r, slot, img, depth_k, depth_b, project_w, hid, mid, moved, conv):
    row = strip * WINDOW + r
    for c in range(0, hid.shape[3], 256):
        at = slice(c, c + 256)
        for j0 in range(0, 8, 4):
            total = None
            for u in range(3):
                part = None
                for v in range(3):
                    term = hid[row + u, j0 + v : j0 + v + 4, :, at] * depth_k[u * 3 + v : u * 3 + v + 1, at][None]
                    part = term if part is None else part + term
                part = part.astype(F32)
                total = part if total is None else total + part
            total = total + depth_b[:, at][None]
            mid[j0 * 16 : j0 * 16 + 64, at] = gelu_bf16(total).reshape(64, 256)
    put_halves(moved, slice(0, 128), dot(mid[...], project_w[...]))
    base = img[row + 1].astype(F32)
    for s in range(16):
        value = strided(moved, s, 8, 16) + base[s * 8 : s * 8 + 8]
        conv[slot, s, pl.ds(pl.multiple_of(r * 8, 8), 8), :] = value


def whole_wait(buf, chunk, sem):
    part = buf.at[chunk, pl.ds(0, PEERS)]
    pltpu.make_async_copy(part, part, sem.at[chunk]).wait()


def block_kernel(
    img, left, right, masks, bn_gain, bn_shift, expand_w, expand_b, depth_k, depth_b, project_w,
    gain0, wq0, wk0, wv0, wo0, gain1, wq1, wk1, wv1, wo1, out,
    rowbuf, hid, mid, moved, conv, obuf, placed, send, recv, reply, back,
    send_sem, recv_sem, reply_sem, back_sem,
):
    cols = lax.axis_size("col")
    me = lax.axis_index("row") * cols + lax.axis_index("col")
    barrier = pltpu.get_barrier_semaphore()

    def peer_of(o):
        return lax.rem(me + o, PEERS + 1)

    def place_of(peer):
        return (lax.div(peer, cols), lax.rem(peer, cols))

    def greet(o, _):
        pl.semaphore_signal(
            barrier, inc=1, device_id=place_of(peer_of(o)), device_id_type=pl.DeviceIdType.MESH
        )
        return 0

    lax.fori_loop(1, PEERS + 1, greet, 0)

    def scatter(chunk, src, dst, src_sem, dst_sem):
        def push(o, _):
            peer = peer_of(o)
            pltpu.make_async_remote_copy(
                src_ref=src.at[chunk, peer],
                dst_ref=dst.at[chunk, me],
                send_sem=src_sem.at[chunk],
                recv_sem=dst_sem.at[chunk],
                device_id=place_of(peer),
                device_id_type=pl.DeviceIdType.MESH,
            ).start()
            return 0

        lax.fori_loop(1, PEERS + 1, push, 0)
        dst[chunk, me] = src[chunk, me]

    edge_low = masks[0]
    edge_high = masks[1]

    def hide(row, _):
        hidden_row(
            row, img, left, right, bn_gain, bn_shift, expand_w, expand_b, edge_low, edge_high, rowbuf, hid
        )
        return 0

    lax.fori_loop(0, 34, hide, 0)
    for c in range(0, hid.shape[3], 256):
        hid[0, :, :, c : c + 256] = hid[0, :, :, c : c + 256] * masks[2][None]
        hid[33, :, :, c : c + 256] = hid[33, :, :, c : c + 256] * masks[3][None]

    pl.semaphore_wait(barrier, PEERS)

    def one_half(half, _):
        def mix(i, _):
            p = lax.div(i, 8)
            mix_row(
                p * 2 + half, lax.rem(i, 8), p, img, depth_k, depth_b, project_w, hid, mid, moved, conv
            )
            return 0

        lax.fori_loop(0, 16, mix, 0)

        def attend_chunk(m, _):
            chunk = half * 4 + m
            x = jnp.concatenate([conv[w // 4, (w % 4) * 4 + m] for w in range(8)], axis=0)
            value = window_attend(x, gain0[...], wq0[...], wk0[...], wv0[...], wo0[...])
            put_halves(obuf, slice(0, 512), value)
            for d in range(PEERS + 1):
                block = [strided(obuf, 2 * d + e, 8, 64) for e in range(2)]
                send[chunk, d] = jnp.concatenate(block, axis=0).astype(BF16)
            scatter(chunk, send, recv, send_sem, recv_sem)
            return 0

        lax.fori_loop(0, 4, attend_chunk, 0)
        return 0

    lax.fori_loop(0, 2, one_half, 0)

    def grid_chunk(chunk, _):
        whole_wait(recv, chunk, recv_sem)
        blocks = recv[chunk].astype(F32)
        done = [
            set_attend(
                blocks[:, e * 8 : e * 8 + 8].reshape(256, 256), gain1[...], wq1[...], wk1[...], wv1[...], wo1[...]
            ).reshape(32, 8, 256)
            for e in range(2)
        ]
        reply[chunk] = jnp.concatenate(done, axis=1).astype(BF16)
        scatter(chunk, reply, back, reply_sem, back_sem)
        return 0

    lax.fori_loop(0, CHUNKS, grid_chunk, 0)

    def finish(chunk, _):
        whole_wait(back, chunk, back_sem)
        half = lax.div(chunk, 4)
        m = lax.rem(chunk, 4)
        put_halves(obuf, slice(0, 512), back[chunk].astype(F32).reshape(512, 256))
        for w in range(8):
            value = strided(obuf, w, 64, 8).reshape(8, 8, 256)
            rows = pl.ds((w // 4) * 16 + half * 8, 8)
            placed[rows, pl.ds(pl.multiple_of((w % 4) * 32 + m * 8, 8), 8), :] = value
        return 0

    lax.fori_loop(0, CHUNKS, finish, 0)

    def store(row, _):
        out[row] = placed[row].astype(BF16)
        return 0

    lax.fori_loop(0, 32, store, 0)

    def drain(chunk, _):
        whole_wait(send, chunk, send_sem)
        whole_wait(reply, chunk, reply_sem)
        return 0

    lax.fori_loop(0, CHUNKS, drain, 0)


def shift_pair(first, last, axis):
    count = lax.axis_size(axis)
    ends = count - 1
    before = lax.ppermute(last, axis, [(i, i + 1) for i in range(ends)])
    after = lax.ppermute(first, axis, [(i + 1, i) for i in range(ends)])
    return before, after


def halo(image):
    top, bottom = shift_pair(image[:1], image[-1:], "row")
    img = jnp.concatenate([top, image, bottom], axis=0)
    left, right = shift_pair(img[:, 0], img[:, -1], "col")
    return img, left.astype(F32), right.astype(F32)


def edge_masks():
    row = lax.axis_index("row")
    col = lax.axis_index("col")
    s = jnp.arange(16)[:, None]
    low = jnp.where((col == 0) & (s == 0), 0.0, 1.0)
    high = jnp.where((col == lax.axis_size("col") - 1) & (s == 15), 0.0, 1.0)
    top = jnp.where(row == 0, 0.0, 1.0) * jnp.ones((16, 1))
    bottom = jnp.where(row == lax.axis_size("row") - 1, 0.0, 1.0) * jnp.ones((16, 1))
    masks = jnp.stack([low, high, top, bottom]).astype(BF16)
    return jnp.broadcast_to(masks, (4, 16, 256))


def split_weights(norm_gain, qkv_weight, out_weight, s):
    chans = qkv_weight.shape[1]
    w = qkv_weight[s]
    return (
        norm_gain[s][None],
        w[:, :chans].T,
        w[:, chans : 2 * chans],
        w[:, 2 * chans :].T,
        out_weight[s],
    )


PEERS = 31
CHUNKS = 8
VMEM = pl.BlockSpec(memory_space=pltpu.VMEM)


def per_device_fast(
    image, bn_gain, bn_shift, expand_weight, expand_bias, depth_kernel, depth_bias, project_weight,
    norm_gain, qkv_weight, out_weight,
):
    wide = expand_weight.shape[1]
    img, left, right = halo(image)
    masks = edge_masks()
    blocks = pltpu.VMEM((CHUNKS, PEERS + 1, 16, 256), BF16)
    sems = pltpu.SemaphoreType.DMA((CHUNKS,))
    return pl.pallas_call(
        block_kernel,
        out_shape=jax.ShapeDtypeStruct(image.shape, BF16),
        in_specs=[VMEM] * 21,
        out_specs=VMEM,
        scratch_shapes=[
            pltpu.VMEM((2, 144, 128), F32),
            pltpu.VMEM((34, 10, 16, wide), BF16),
            pltpu.VMEM((128, wide), BF16),
            pltpu.VMEM((2, 128, 128), F32),
            pltpu.VMEM((2, 16, 64, 256), F32),
            pltpu.VMEM((2, 512, 128), F32),
            pltpu.VMEM(image.shape, F32),
            blocks, blocks, blocks, blocks,
            sems, sems, sems, sems,
        ],
        compiler_params=pltpu.CompilerParams(
            collective_id=0, has_side_effects=True, vmem_limit_bytes=56 * 1024 * 1024
        ),
    )(
        img, left, right, masks, bn_gain[None], bn_shift[None], expand_weight, expand_bias[None],
        depth_kernel.reshape(9, wide), depth_bias[None], project_weight,
        *split_weights(norm_gain, qkv_weight, out_weight, 0),
        *split_weights(norm_gain, qkv_weight, out_weight, 1),
    )


def solution(mesh):
    in_specs = (P("row", "col", None), P(), P(), P(), P(), P(), P(), P(), P(), P(), P())
    out_specs = P("row", "col", None)
    fast = mesh.shape["row"] == 8 and mesh.shape["col"] == 4
    return jax.shard_map(
        per_device_fast if fast else per_device, mesh=mesh, in_specs=in_specs, out_specs=out_specs, check_vma=False
    )
```

```python
import math

import jax
import jax.numpy as jnp
from jax import lax
from jax.experimental import pallas as pl
from jax.experimental.pallas import tpu as pltpu
from jax.sharding import PartitionSpec as P

HEADS = 8
WINDOW = 8
GRID_SIDE = 16


def padded(cells, sides, width):
    for axis, dim in sides:
        count = lax.axis_size(axis)
        ends = count - 1
        head = lax.slice_in_dim(cells, 0, width, axis=dim)
        tail = lax.slice_in_dim(cells, cells.shape[dim] - width, cells.shape[dim], axis=dim)
        cells = jnp.concatenate(
            [
                lax.ppermute(tail, axis, [(i, (i + 1) % count) for i in range(ends)]),
                cells,
                lax.ppermute(head, axis, [((i + 1) % count, i) for i in range(ends)]),
            ],
            axis=dim,
        )
    return cells


def layer_norm(values, gain):
    mean = jnp.mean(values, axis=-1, keepdims=True)
    centred = values - mean
    spread = jnp.mean(centred * centred, axis=-1, keepdims=True)
    return centred * lax.rsqrt(spread + 1e-05) * gain


def expand_pixels(pixels, bn_gain, bn_shift, expand_weight, expand_bias):
    shape = pixels.shape
    normed = (pixels.astype(jnp.float32) * bn_gain + bn_shift).astype(jnp.bfloat16)
    hidden = (
        jnp.dot(normed.reshape(-1, shape[-1]), expand_weight, preferred_element_type=jnp.float32)
        + expand_bias
    )
    return jax.nn.gelu(hidden).astype(jnp.bfloat16).reshape(shape[:-1] + (expand_weight.shape[1],))


def depth_project(framed, residual, depth_kernel, depth_bias, project_weight):
    height = residual.shape[0]
    width = residual.shape[1]
    kernel = depth_kernel.astype(jnp.float32)
    total = jnp.zeros((height, width, framed.shape[2]), jnp.float32)
    for down in range(3):
        for across in range(3):
            total = (
                total
                + framed[down : down + height, across : across + width].astype(jnp.float32)
                * kernel[down, across]
            )
    middle = jax.nn.gelu(total + depth_bias).astype(jnp.bfloat16)
    moved = jnp.dot(
        middle.reshape(height * width, -1), project_weight, preferred_element_type=jnp.float32
    )
    return (residual.astype(jnp.float32) + moved.reshape(height, width, -1)).astype(jnp.bfloat16)


def attend(tokens, gain, qkv_weight, out_weight):
    groups, length, chans = tokens.shape
    values = tokens.astype(jnp.float32)
    normed = layer_norm(values, gain).astype(jnp.bfloat16)
    proj = jnp.dot(
        normed.reshape(groups * length, chans), qkv_weight, preferred_element_type=jnp.float32
    ).astype(jnp.bfloat16)
    proj = proj.reshape(groups, length, 3, HEADS, chans // HEADS)
    query = proj[:, :, 0]
    keys = proj[:, :, 1]
    vals = proj[:, :, 2]
    scores = jnp.einsum("gqhd,gkhd->ghqk", query, keys, preferred_element_type=jnp.float32) * (
        chans // HEADS
    ) ** (-0.5)
    top = jnp.max(scores, axis=-1, keepdims=True)
    weights = jnp.exp(scores - top)
    probs = (weights / jnp.sum(weights, axis=-1, keepdims=True)).astype(jnp.bfloat16)
    mixed = jnp.einsum("ghqk,gkhd->gqhd", probs, vals, preferred_element_type=jnp.float32).astype(
        jnp.bfloat16
    )
    moved = jnp.dot(
        mixed.reshape(groups * length, chans), out_weight, preferred_element_type=jnp.float32
    )
    return (values + moved.reshape(groups, length, chans)).astype(jnp.bfloat16)


def attend_batched(tokens, gain, qkv_weight, out_weight, wanted):
    groups = tokens.shape[0]
    per_step = math.gcd(groups, wanted)
    stacked = tokens.reshape((groups // per_step, per_step) + tokens.shape[1:])

    def one_batch(batch):
        return attend(batch, gain, qkv_weight, out_weight)

    return lax.map(one_batch, stacked).reshape(tokens.shape)


def per_device(
    image,
    bn_gain,
    bn_shift,
    expand_weight,
    expand_bias,
    depth_kernel,
    depth_bias,
    project_weight,
    norm_gain,
    qkv_weight,
    out_weight,
):
    rows_dev, cols_dev, chans = image.shape
    row_count = lax.axis_size("row")
    col_count = lax.axis_size("col")
    strips = rows_dev // WINDOW

    def expand_strip(index):
        piece = lax.dynamic_slice_in_dim(image, index * WINDOW, WINDOW, 0)
        return expand_pixels(piece, bn_gain, bn_shift, expand_weight, expand_bias)

    hidden = lax.map(expand_strip, jnp.arange(strips)).reshape(rows_dev, cols_dev, -1)
    framed_all = padded(hidden, (("row", 0), ("col", 1)), 1)

    def mix_strip(index):
        framed = lax.dynamic_slice_in_dim(framed_all, index * WINDOW, WINDOW + 2, 0)
        residual = lax.dynamic_slice_in_dim(image, index * WINDOW, WINDOW, 0)
        return depth_project(framed, residual, depth_kernel, depth_bias, project_weight)

    after_conv = lax.map(mix_strip, jnp.arange(strips)).reshape(rows_dev, cols_dev, chans)
    windows = after_conv.reshape(
        rows_dev // WINDOW, WINDOW, cols_dev // WINDOW, WINDOW, chans
    ).transpose(0, 2, 1, 3, 4)
    windows = windows.reshape(-1, WINDOW * WINDOW, chans)
    windows = attend_batched(windows, norm_gain[0], qkv_weight[0], out_weight[0], 16)
    after_block = windows.reshape(
        rows_dev // WINDOW, cols_dev // WINDOW, WINDOW, WINDOW, chans
    ).transpose(0, 2, 1, 3, 4)
    after_block = after_block.reshape(rows_dev, cols_dev, chans)
    rep_row = GRID_SIDE // row_count
    rep_col = GRID_SIDE // col_count
    low_row = rows_dev // GRID_SIDE
    low_col = cols_dev // GRID_SIDE
    items = low_row * low_col
    local = rep_row * rep_col
    devices = row_count * col_count
    arranged = after_block.reshape(
        rep_row, row_count, low_row, rep_col, col_count, low_col, chans
    ).transpose(1, 4, 2, 5, 0, 3, 6)
    outgoing = arranged.reshape(devices, 1, items, local, chans)
    received = lax.all_to_all(outgoing, ("row", "col"), split_axis=0, concat_axis=1, tiled=True)
    count = received.shape[2]
    tokens = (
        received.reshape(devices, count, local, chans)
        .transpose(1, 0, 2, 3)
        .reshape(count, devices * local, chans)
    )
    done = attend_batched(tokens, norm_gain[1], qkv_weight[1], out_weight[1], 2)
    reply = (
        done.reshape(count, devices, local, chans)
        .transpose(1, 0, 2, 3)
        .reshape(1, devices, count, local, chans)
    )
    returned = lax.all_to_all(reply, ("row", "col"), split_axis=1, concat_axis=0, tiled=True)
    placed = returned.reshape(
        row_count, col_count, low_row, low_col, rep_row, rep_col, chans
    ).transpose(4, 0, 2, 5, 1, 3, 6)
    return placed.reshape(rows_dev, cols_dev, chans)


NT = (((1,), (1,)), ((), ()))
TN = (((0,), (0,)), ((), ()))
F32 = jnp.float32
BF16 = jnp.bfloat16
GELU_IN = math.sqrt(2.0 / math.pi)


def dot(a, b, dims=(((1,), (0,)), ((), ()))):
    return lax.dot_general(a, b, dims, preferred_element_type=F32)


def gelu_bf16(x):
    x = x.astype(BF16)
    inner = x * (x * x * BF16(GELU_IN * 0.044715) + BF16(GELU_IN))
    half = x * BF16(0.5)
    return half + half * jnp.tanh(inner)


def norm_rows(x, gain):
    mean = jnp.mean(x, axis=-1, keepdims=True)
    centred = x - mean
    spread = jnp.mean(centred * centred, axis=-1, keepdims=True)
    return (centred * lax.rsqrt(spread + 1e-05) * gain).astype(BF16)


def head_rows(q_t, head, size):
    chans, width = q_t.shape
    parts = []
    if head:
        parts.append(jnp.zeros((head * size, width), BF16))
    parts.append(q_t[head * size : (head + 1) * size])
    if (head + 1) * size < chans:
        parts.append(jnp.zeros((chans - (head + 1) * size, width), BF16))
    return jnp.concatenate(parts, axis=0)


def project_qkv(x, gain, wq_t, wk, wv_t, size):
    ln = norm_rows(x, gain)
    scale = math.log2(math.e) / math.sqrt(size)
    q_t = (dot(wq_t, ln, NT) * scale).astype(BF16)
    k = dot(ln, wk).astype(BF16)
    v_t = dot(wv_t, ln, NT).astype(BF16)
    return q_t, k, v_t


def window_attend(x, gain, wq_t, wk, wv_t, wo):
    tokens, chans = x.shape
    size = chans // HEADS
    q_t, k, v_t = project_qkv(x, gain, wq_t, wk, wv_t, size)
    lane = lax.broadcasted_iota(jnp.int32, (64, 256), 1)
    low = (lane % 128) < 64
    low_mask = low.astype(F32).astype(BF16)
    high_mask = (1.0 - low.astype(F32)).astype(BF16)
    ones = jnp.ones((16, 128), BF16)
    columns = []
    for pair in range(tokens // 128):
        at = slice(pair * 128, pair * 128 + 128)
        k_p = k[at]
        mixed = []
        for h in range(0, HEADS, 2):
            rhs = jnp.concatenate(
                [head_rows(q_t[:, at], h, size), head_rows(q_t[:, at], h + 1, size)], axis=1
            )
            s = dot(k_p, rhs)
            s = jnp.where(low, s[:64], s[64:])
            p = jnp.exp2(s - jnp.max(s, axis=0, keepdims=True)).astype(BF16)
            p = jnp.concatenate([p * low_mask, p * high_mask], axis=0)
            lhs = jnp.concatenate([v_t[h * size : (h + 2) * size, at], ones], axis=0)
            o = dot(lhs, p)
            inv = 1.0 / o[2 * size : 2 * size + 1]
            mixed.append((o[:size, :128] * inv[:, :128]).astype(BF16))
            mixed.append((o[size : 2 * size, 128:] * inv[:, 128:]).astype(BF16))
        columns.append(jnp.concatenate(mixed, axis=0))
    mixed_t = jnp.concatenate(columns, axis=1)
    return x + dot(mixed_t, wo, TN)


def set_attend(x, gain, wq_t, wk, wv_t, wo):
    tokens, chans = x.shape
    size = chans // HEADS
    q_t, k, v_t = project_qkv(x, gain, wq_t, wk, wv_t, size)
    ones = jnp.ones((16, tokens), BF16)
    mixed = []
    for h in range(HEADS):
        s = dot(k, head_rows(q_t, h, size))
        p = jnp.exp2(s - jnp.max(s, axis=0, keepdims=True)).astype(BF16)
        lhs = jnp.concatenate([v_t[h * size : (h + 1) * size], ones], axis=0)
        o = dot(lhs, p)
        mixed.append((o[:size] * (1.0 / o[size : size + 1])).astype(BF16))
    return x + dot(jnp.concatenate(mixed, axis=0), wo, TN)


def put_halves(ref, rows, value):
    ref[0, rows, :] = value[:, :128]
    ref[1, rows, :] = value[:, 128:]


def strided(ref, start, count, stride):
    rows = pl.ds(start, count, stride=stride)
    return jnp.concatenate([ref[0, rows, :], ref[1, rows, :]], axis=1)


def hidden_row(
    row, cells, left, right, bn_gain, bn_shift, expand_w, expand_b, edge_low, edge_high, rowbuf, hid
):
    gain = bn_gain[...]
    shift = bn_shift[...]
    put_halves(rowbuf, slice(8, 136), cells.astype(F32) * gain + shift)
    put_halves(rowbuf, slice(7, 8), left[pl.ds(row, 1), :] * gain + shift)
    put_halves(rowbuf, slice(136, 137), right[pl.ds(row, 1), :] * gain + shift)
    planes = [strided(rowbuf, 7 + j, 16, 8) for j in range(10)]
    normed = jnp.concatenate(planes, axis=0).astype(BF16)
    for c in range(0, expand_w.shape[1], 256):
        h = dot(normed, expand_w[:, c : c + 256]) + expand_b[:, c : c + 256]
        h = gelu_bf16(h).reshape(10, 16, 256)
        hid[row, 0, :, c : c + 256] = h[0] * edge_low
        hid[row, 1:9, :, c : c + 256] = h[1:9]
        hid[row, 9, :, c : c + 256] = h[9] * edge_high


def mix_row(strip, r, slot, img, depth_k, depth_b, project_w, hid, mid, moved, conv):
    row = strip * WINDOW + r
    for c in range(0, hid.shape[3], 256):
        at = slice(c, c + 256)
        for j0 in range(0, 8, 4):
            total = None
            for u in range(3):
                part = None
                for v in range(3):
                    term = hid[row + u, j0 + v : j0 + v + 4, :, at] * depth_k[u, v : v + 1, at][None]
                    part = term if part is None else part + term
                part = part.astype(F32)
                total = part if total is None else total + part
            total = total + depth_b[:, at][None]
            mid[j0 * 16 : j0 * 16 + 64, at] = gelu_bf16(total).reshape(64, 256)
    put_halves(moved, slice(0, 128), dot(mid[...], project_w[...]))
    base = img[row].astype(F32)
    for s in range(16):
        value = strided(moved, s, 8, 16) + base[s * 8 : s * 8 + 8]
        conv[slot, s, pl.ds(pl.multiple_of(r * 8, 8), 8), :] = value


def whole_wait(buf, chunk, sem):
    part = buf.at[chunk, pl.ds(0, PEERS)]
    pltpu.make_async_copy(part, part, sem.at[chunk]).wait()


def block_kernel(
    img, bn_gain, bn_shift, expand_w, expand_b, depth_k, depth_b, project_w,
    norm_gain, qkv_w, out_w, out,
    rowbuf, hid, mid, moved, conv, obuf, placed, rows_in, ends_out, ends_in, turned,
    send, recv, reply, back, halo_sem, send_sem, recv_sem, reply_sem, back_sem,
):
    cols = lax.axis_size("col")
    me = lax.axis_index("row") * cols + lax.axis_index("col")
    barrier = pltpu.get_barrier_semaphore()

    def peer_of(o):
        return lax.rem(me + o, PEERS + 1)

    def place_of(peer):
        return (lax.div(peer, cols), lax.rem(peer, cols))

    def greet(o, _):
        pl.semaphore_signal(
            barrier, inc=1, device_id=place_of(peer_of(o)), device_id_type=pl.DeviceIdType.MESH
        )
        return 0

    lax.fori_loop(1, PEERS + 1, greet, 0)

    def scatter(chunk, src, dst, src_sem, dst_sem):
        def push(o, _):
            peer = peer_of(o)
            pltpu.make_async_remote_copy(
                src_ref=src.at[chunk, peer],
                dst_ref=dst.at[chunk, me],
                send_sem=src_sem.at[chunk],
                recv_sem=dst_sem.at[chunk],
                device_id=place_of(peer),
                device_id_type=pl.DeviceIdType.MESH,
            ).start()
            return 0

        lax.fori_loop(1, PEERS + 1, push, 0)
        dst[chunk, me] = src[chunk, me]

    my_row = lax.axis_index("row")
    my_col = lax.axis_index("col")
    row_count = lax.axis_size("row")
    pl.semaphore_wait(barrier, PEERS)

    def ring_copy(src, dst, sem, place):
        return pltpu.make_async_remote_copy(
            src_ref=src,
            dst_ref=dst,
            send_sem=halo_sem.at[sem],
            recv_sem=halo_sem.at[sem + 1],
            device_id=place,
            device_id_type=pl.DeviceIdType.MESH,
        )

    below = lax.rem(my_row + 1, row_count)
    above = lax.rem(my_row + row_count - 1, row_count)
    after = lax.rem(my_col + 1, cols)
    before = lax.rem(my_col + cols - 1, cols)
    down = ring_copy(img.at[31], rows_in.at[0], 0, (below, my_col))
    up = ring_copy(img.at[0], rows_in.at[1], 2, (above, my_col))
    down.start()
    up.start()
    chans = img.shape[2]
    for n in range(2):
        ends_out[n, 32:40, :] = jnp.zeros((8, chans), F32)
    for s in range(2):
        for n in range(2):
            part = qkv_w[s, :, n * 2 * chans : (n * 2 + 1) * chans]
            turned[s, n] = part.astype(F32).T.astype(BF16)
    for row in range(32):
        cells = img[row].astype(F32)
        ends_out[0, row + 1 : row + 2, :] = cells[:1]
        ends_out[1, row + 1 : row + 2, :] = cells[127:]
    down.wait()
    up.wait()
    for n, row in ((0, 0), (1, 33)):
        cells = rows_in[n].astype(F32)
        ends_out[0, row : row + 1, :] = cells[:1]
        ends_out[1, row : row + 1, :] = cells[127:]
    forth = ring_copy(ends_out.at[1], ends_in.at[0], 4, (my_row, after))
    aft = ring_copy(ends_out.at[0], ends_in.at[1], 6, (my_row, before))
    forth.start()
    aft.start()
    spot = lax.broadcasted_iota(jnp.int32, (16, chans), 0)
    edge_low = jnp.where((spot == 0) & (my_col == 0), 0.0, 1.0).astype(BF16)
    edge_high = jnp.where((spot == 15) & (my_col == cols - 1), 0.0, 1.0).astype(BF16)
    every = jnp.ones((16, chans), F32)
    edge_top = jnp.where(my_row == 0, 0.0, every).astype(BF16)
    edge_bottom = jnp.where(my_row == row_count - 1, 0.0, every).astype(BF16)
    forth.wait()
    aft.wait()

    def hide_row(row, cells, slot):
        hidden_row(
            row, cells, ends_in.at[0], ends_in.at[1], bn_gain, bn_shift, expand_w, expand_b, edge_low, edge_high,
            rowbuf.at[slot], hid,
        )

    def hide(i, _):
        for k in range(2):
            hide_row(2 * i + k + 1, img[2 * i + k], k)
        return 0

    lax.fori_loop(0, 16, hide, 0)
    hide_row(0, rows_in[0], 0)
    hide_row(33, rows_in[1], 1)
    for c in range(0, hid.shape[3], 256):
        hid[0, :, :, c : c + 256] = hid[0, :, :, c : c + 256] * edge_top[None]
        hid[33, :, :, c : c + 256] = hid[33, :, :, c : c + 256] * edge_bottom[None]

    def weights(s):
        return (
            norm_gain[s : s + 1, :],
            turned[s, 0],
            qkv_w[s, :, chans : 2 * chans],
            turned[s, 1],
            out_w[s],
        )

    def one_half(half, _):
        def mix(i, _):
            p = lax.div(i, 4)
            for k in range(2):
                mix_row(
                    p * 2 + half, lax.rem(i, 4) * 2 + k, p, img, depth_k, depth_b, project_w, hid,
                    mid.at[k], moved.at[k], conv,
                )
            return 0

        lax.fori_loop(0, 8, mix, 0)

        def attend_chunk(m, _):
            chunk = half * 4 + m
            x = jnp.concatenate([conv[w // 4, (w % 4) * 4 + m] for w in range(8)], axis=0)
            value = window_attend(x, *weights(0))
            put_halves(obuf, slice(0, 512), value)
            for d in range(PEERS + 1):
                block = [strided(obuf, 2 * d + e, 8, 64) for e in range(2)]
                send[chunk, d] = jnp.concatenate(block, axis=0).astype(BF16)
            scatter(chunk, send, recv, send_sem, recv_sem)
            return 0

        lax.fori_loop(0, 4, attend_chunk, 0)
        return 0

    lax.fori_loop(0, 2, one_half, 0)

    def grid_chunk(chunk, _):
        whole_wait(recv, chunk, recv_sem)
        blocks = recv[chunk].astype(F32)
        done = [
            set_attend(
                blocks[:, e * 8 : e * 8 + 8].reshape(256, 256), *weights(1)
            ).reshape(32, 8, 256)
            for e in range(2)
        ]
        reply[chunk] = jnp.concatenate(done, axis=1).astype(BF16)
        scatter(chunk, reply, back, reply_sem, back_sem)
        return 0

    lax.fori_loop(0, CHUNKS, grid_chunk, 0)

    def finish(chunk, _):
        whole_wait(back, chunk, back_sem)
        half = lax.div(chunk, 4)
        m = lax.rem(chunk, 4)
        put_halves(obuf, slice(0, 512), back[chunk].astype(F32).reshape(512, 256))
        for w in range(8):
            value = strided(obuf, w, 64, 8).reshape(8, 8, 256)
            rows = pl.ds((w // 4) * 16 + half * 8, 8)
            placed[rows, pl.ds(pl.multiple_of((w % 4) * 32 + m * 8, 8), 8), :] = value
        return 0

    def finish_half(half, _):
        lax.fori_loop(half * 4, half * 4 + 4, finish, 0)

        def store(i, _):
            row = lax.div(i, 8) * 16 + half * 8 + lax.rem(i, 8)
            out[row] = placed[row].astype(BF16)
            return 0

        lax.fori_loop(0, 16, store, 0)
        return 0

    lax.fori_loop(0, 2, finish_half, 0)

    def drain(chunk, _):
        whole_wait(send, chunk, send_sem)
        whole_wait(reply, chunk, reply_sem)
        return 0

    lax.fori_loop(0, CHUNKS, drain, 0)


PEERS = 31
CHUNKS = 8
VMEM = pl.BlockSpec(memory_space=pltpu.VMEM)


def per_device_fast(
    image, bn_gain, bn_shift, expand_weight, expand_bias, depth_kernel, depth_bias, project_weight,
    norm_gain, qkv_weight, out_weight,
):
    wide = expand_weight.shape[1]
    blocks = pltpu.VMEM((CHUNKS, PEERS + 1, 16, 256), BF16)
    sems = pltpu.SemaphoreType.DMA((CHUNKS,))
    return pl.pallas_call(
        block_kernel,
        out_shape=jax.ShapeDtypeStruct(image.shape, BF16),
        in_specs=[VMEM] * 11,
        out_specs=VMEM,
        scratch_shapes=[
            pltpu.VMEM((2, 2, 144, 128), F32),
            pltpu.VMEM((34, 10, 16, wide), BF16),
            pltpu.VMEM((2, 128, wide), BF16),
            pltpu.VMEM((2, 2, 128, 128), F32),
            pltpu.VMEM((2, 16, 64, 256), F32),
            pltpu.VMEM((2, 512, 128), F32),
            pltpu.VMEM(image.shape, F32),
            pltpu.VMEM((2, 128, 256), BF16),
            pltpu.VMEM((2, 40, 256), F32),
            pltpu.VMEM((2, 40, 256), F32),
            pltpu.VMEM((2, 2, 256, 256), BF16),
            blocks, blocks, blocks, blocks,
            sems, sems, sems, sems, sems,
        ],
        compiler_params=pltpu.CompilerParams(
            collective_id=0, has_side_effects=True, vmem_limit_bytes=56 * 1024 * 1024
        ),
    )(
        image, bn_gain[None], bn_shift[None], expand_weight, expand_bias[None],
        depth_kernel, depth_bias[None], project_weight, norm_gain, qkv_weight, out_weight,
    )


def solution(mesh):
    in_specs = (P("row", "col", None), P(), P(), P(), P(), P(), P(), P(), P(), P(), P())
    out_specs = P("row", "col", None)
    fast = mesh.shape["row"] == 8 and mesh.shape["col"] == 4
    return jax.shard_map(
        per_device_fast if fast else per_device, mesh=mesh, in_specs=in_specs, out_specs=out_specs, check_vma=False
    )
```

```python
import math

import jax
import jax.numpy as jnp
from jax import lax
from jax.experimental import pallas as pl
from jax.experimental.pallas import tpu as pltpu
from jax.sharding import PartitionSpec as P

HEADS = 8
WINDOW = 8
GRID_SIDE = 16


def padded(cells, sides, width):
    for axis, dim in sides:
        count = lax.axis_size(axis)
        ends = count - 1
        head = lax.slice_in_dim(cells, 0, width, axis=dim)
        tail = lax.slice_in_dim(cells, cells.shape[dim] - width, cells.shape[dim], axis=dim)
        cells = jnp.concatenate(
            [
                lax.ppermute(tail, axis, [(i, (i + 1) % count) for i in range(ends)]),
                cells,
                lax.ppermute(head, axis, [((i + 1) % count, i) for i in range(ends)]),
            ],
            axis=dim,
        )
    return cells


def layer_norm(values, gain):
    mean = jnp.mean(values, axis=-1, keepdims=True)
    centred = values - mean
    spread = jnp.mean(centred * centred, axis=-1, keepdims=True)
    return centred * lax.rsqrt(spread + 1e-05) * gain


def expand_pixels(pixels, bn_gain, bn_shift, expand_weight, expand_bias):
    shape = pixels.shape
    normed = (pixels.astype(jnp.float32) * bn_gain + bn_shift).astype(jnp.bfloat16)
    hidden = (
        jnp.dot(normed.reshape(-1, shape[-1]), expand_weight, preferred_element_type=jnp.float32)
        + expand_bias
    )
    return jax.nn.gelu(hidden).astype(jnp.bfloat16).reshape(shape[:-1] + (expand_weight.shape[1],))


def depth_project(framed, residual, depth_kernel, depth_bias, project_weight):
    height = residual.shape[0]
    width = residual.shape[1]
    kernel = depth_kernel.astype(jnp.float32)
    total = jnp.zeros((height, width, framed.shape[2]), jnp.float32)
    for down in range(3):
        for across in range(3):
            total = (
                total
                + framed[down : down + height, across : across + width].astype(jnp.float32)
                * kernel[down, across]
            )
    middle = jax.nn.gelu(total + depth_bias).astype(jnp.bfloat16)
    moved = jnp.dot(
        middle.reshape(height * width, -1), project_weight, preferred_element_type=jnp.float32
    )
    return (residual.astype(jnp.float32) + moved.reshape(height, width, -1)).astype(jnp.bfloat16)


def attend(tokens, gain, qkv_weight, out_weight):
    groups, length, chans = tokens.shape
    values = tokens.astype(jnp.float32)
    normed = layer_norm(values, gain).astype(jnp.bfloat16)
    proj = jnp.dot(
        normed.reshape(groups * length, chans), qkv_weight, preferred_element_type=jnp.float32
    ).astype(jnp.bfloat16)
    proj = proj.reshape(groups, length, 3, HEADS, chans // HEADS)
    query = proj[:, :, 0]
    keys = proj[:, :, 1]
    vals = proj[:, :, 2]
    scores = jnp.einsum("gqhd,gkhd->ghqk", query, keys, preferred_element_type=jnp.float32) * (
        chans // HEADS
    ) ** (-0.5)
    top = jnp.max(scores, axis=-1, keepdims=True)
    weights = jnp.exp(scores - top)
    probs = (weights / jnp.sum(weights, axis=-1, keepdims=True)).astype(jnp.bfloat16)
    mixed = jnp.einsum("ghqk,gkhd->gqhd", probs, vals, preferred_element_type=jnp.float32).astype(
        jnp.bfloat16
    )
    moved = jnp.dot(
        mixed.reshape(groups * length, chans), out_weight, preferred_element_type=jnp.float32
    )
    return (values + moved.reshape(groups, length, chans)).astype(jnp.bfloat16)


def attend_batched(tokens, gain, qkv_weight, out_weight, wanted):
    groups = tokens.shape[0]
    per_step = math.gcd(groups, wanted)
    stacked = tokens.reshape((groups // per_step, per_step) + tokens.shape[1:])

    def one_batch(batch):
        return attend(batch, gain, qkv_weight, out_weight)

    return lax.map(one_batch, stacked).reshape(tokens.shape)


def per_device(
    image,
    bn_gain,
    bn_shift,
    expand_weight,
    expand_bias,
    depth_kernel,
    depth_bias,
    project_weight,
    norm_gain,
    qkv_weight,
    out_weight,
):
    rows_dev, cols_dev, chans = image.shape
    row_count = lax.axis_size("row")
    col_count = lax.axis_size("col")
    strips = rows_dev // WINDOW

    def expand_strip(index):
        piece = lax.dynamic_slice_in_dim(image, index * WINDOW, WINDOW, 0)
        return expand_pixels(piece, bn_gain, bn_shift, expand_weight, expand_bias)

    hidden = lax.map(expand_strip, jnp.arange(strips)).reshape(rows_dev, cols_dev, -1)
    framed_all = padded(hidden, (("row", 0), ("col", 1)), 1)

    def mix_strip(index):
        framed = lax.dynamic_slice_in_dim(framed_all, index * WINDOW, WINDOW + 2, 0)
        residual = lax.dynamic_slice_in_dim(image, index * WINDOW, WINDOW, 0)
        return depth_project(framed, residual, depth_kernel, depth_bias, project_weight)

    after_conv = lax.map(mix_strip, jnp.arange(strips)).reshape(rows_dev, cols_dev, chans)
    windows = after_conv.reshape(
        rows_dev // WINDOW, WINDOW, cols_dev // WINDOW, WINDOW, chans
    ).transpose(0, 2, 1, 3, 4)
    windows = windows.reshape(-1, WINDOW * WINDOW, chans)
    windows = attend_batched(windows, norm_gain[0], qkv_weight[0], out_weight[0], 16)
    after_block = windows.reshape(
        rows_dev // WINDOW, cols_dev // WINDOW, WINDOW, WINDOW, chans
    ).transpose(0, 2, 1, 3, 4)
    after_block = after_block.reshape(rows_dev, cols_dev, chans)
    rep_row = GRID_SIDE // row_count
    rep_col = GRID_SIDE // col_count
    low_row = rows_dev // GRID_SIDE
    low_col = cols_dev // GRID_SIDE
    items = low_row * low_col
    local = rep_row * rep_col
    devices = row_count * col_count
    arranged = after_block.reshape(
        rep_row, row_count, low_row, rep_col, col_count, low_col, chans
    ).transpose(1, 4, 2, 5, 0, 3, 6)
    outgoing = arranged.reshape(devices, 1, items, local, chans)
    received = lax.all_to_all(outgoing, ("row", "col"), split_axis=0, concat_axis=1, tiled=True)
    count = received.shape[2]
    tokens = (
        received.reshape(devices, count, local, chans)
        .transpose(1, 0, 2, 3)
        .reshape(count, devices * local, chans)
    )
    done = attend_batched(tokens, norm_gain[1], qkv_weight[1], out_weight[1], 2)
    reply = (
        done.reshape(count, devices, local, chans)
        .transpose(1, 0, 2, 3)
        .reshape(1, devices, count, local, chans)
    )
    returned = lax.all_to_all(reply, ("row", "col"), split_axis=1, concat_axis=0, tiled=True)
    placed = returned.reshape(
        row_count, col_count, low_row, low_col, rep_row, rep_col, chans
    ).transpose(4, 0, 2, 5, 1, 3, 6)
    return placed.reshape(rows_dev, cols_dev, chans)


NT = (((1,), (1,)), ((), ()))
TN = (((0,), (0,)), ((), ()))
F32 = jnp.float32
BF16 = jnp.bfloat16
GELU_IN = math.sqrt(2.0 / math.pi)


def dot(a, b, dims=(((1,), (0,)), ((), ()))):
    return lax.dot_general(a, b, dims, preferred_element_type=F32)


def gelu_bf16(x):
    x = x.astype(BF16)
    inner = x * (x * x * BF16(GELU_IN * 0.044715) + BF16(GELU_IN))
    half = x * BF16(0.5)
    return half + half * jnp.tanh(inner)


def norm_rows(x, gain):
    mean = jnp.mean(x, axis=-1, keepdims=True)
    centred = x - mean
    spread = jnp.mean(centred * centred, axis=-1, keepdims=True)
    return (centred * lax.rsqrt(spread + 1e-05) * gain).astype(BF16)


def head_rows(q_t, head, size):
    chans, width = q_t.shape
    parts = []
    if head:
        parts.append(jnp.zeros((head * size, width), BF16))
    parts.append(q_t[head * size : (head + 1) * size])
    if (head + 1) * size < chans:
        parts.append(jnp.zeros((chans - (head + 1) * size, width), BF16))
    return jnp.concatenate(parts, axis=0)


def project_qkv(x, gain, wq_t, wk, wv_t, size):
    ln = norm_rows(x, gain)
    scale = math.log2(math.e) / math.sqrt(size)
    q_t = (dot(wq_t, ln, NT) * scale).astype(BF16)
    k = dot(ln, wk).astype(BF16)
    v_t = dot(wv_t, ln, NT).astype(BF16)
    return q_t, k, v_t


def window_attend(x, gain, wq_t, wk, wv_t, wo):
    tokens, chans = x.shape
    size = chans // HEADS
    q_t, k, v_t = project_qkv(x, gain, wq_t, wk, wv_t, size)
    lane = lax.broadcasted_iota(jnp.int32, (64, 256), 1)
    low = (lane % 128) < 64
    low_mask = low.astype(F32).astype(BF16)
    high_mask = (1.0 - low.astype(F32)).astype(BF16)
    ones = jnp.ones((16, 128), BF16)
    columns = []
    for pair in range(tokens // 128):
        at = slice(pair * 128, pair * 128 + 128)
        k_p = k[at]
        mixed = []
        for h in range(0, HEADS, 2):
            rhs = jnp.concatenate(
                [head_rows(q_t[:, at], h, size), head_rows(q_t[:, at], h + 1, size)], axis=1
            )
            s = dot(k_p, rhs)
            s = jnp.where(low, s[:64], s[64:])
            p = jnp.exp2((s - jnp.max(s, axis=0, keepdims=True)).astype(BF16))
            p = jnp.concatenate([p * low_mask, p * high_mask], axis=0)
            lhs = jnp.concatenate([v_t[h * size : (h + 2) * size, at], ones], axis=0)
            o = dot(lhs, p)
            inv = 1.0 / o[2 * size : 2 * size + 1]
            mixed.append((o[:size, :128] * inv[:, :128]).astype(BF16))
            mixed.append((o[size : 2 * size, 128:] * inv[:, 128:]).astype(BF16))
        columns.append(jnp.concatenate(mixed, axis=0))
    mixed_t = jnp.concatenate(columns, axis=1)
    return x + dot(mixed_t, wo, TN)


def set_attend(x, gain, wq_t, wk, wv_t, wo):
    tokens, chans = x.shape
    size = chans // HEADS
    q_t, k, v_t = project_qkv(x, gain, wq_t, wk, wv_t, size)
    ones = jnp.ones((16, tokens), BF16)
    mixed = []
    for h in range(HEADS):
        s = dot(k, head_rows(q_t, h, size))
        p = jnp.exp2((s - jnp.max(s, axis=0, keepdims=True)).astype(BF16))
        lhs = jnp.concatenate([v_t[h * size : (h + 1) * size], ones], axis=0)
        o = dot(lhs, p)
        mixed.append((o[:size] * (1.0 / o[size : size + 1])).astype(BF16))
    return x + dot(jnp.concatenate(mixed, axis=0), wo, TN)


def put_halves(ref, rows, value):
    ref[0, rows, :] = value[:, :128]
    ref[1, rows, :] = value[:, 128:]


def strided(ref, start, count, stride):
    rows = pl.ds(start, count, stride=stride)
    return jnp.concatenate([ref[0, rows, :], ref[1, rows, :]], axis=1)


def hidden_row(
    row, cells, left, right, bn_gain, bn_shift, expand_w, expand_b, edge_low, edge_high, rowbuf, hid
):
    gain = bn_gain[...]
    shift = bn_shift[...]
    put_halves(rowbuf, slice(8, 136), cells.astype(F32) * gain + shift)
    put_halves(rowbuf, slice(7, 8), left[pl.ds(row, 1), :] * gain + shift)
    put_halves(rowbuf, slice(136, 137), right[pl.ds(row, 1), :] * gain + shift)
    planes = [strided(rowbuf, 7 + j, 16, 8) for j in range(10)]
    normed = jnp.concatenate(planes, axis=0).astype(BF16)
    for c in range(0, expand_w.shape[1], 256):
        h = dot(normed, expand_w[:, c : c + 256]) + expand_b[:, c : c + 256]
        h = gelu_bf16(h).reshape(10, 16, 256)
        hid[row, 0, :, c : c + 256] = h[0] * edge_low
        hid[row, 1:9, :, c : c + 256] = h[1:9]
        hid[row, 9, :, c : c + 256] = h[9] * edge_high


def mix_row(strip, r, slot, img, taps, depth_b, project_w, hid, mid, moved, conv):
    row = strip * WINDOW + r
    for c in range(0, hid.shape[3], 256):
        at = slice(c, c + 256)
        for j0 in range(0, 8, 4):
            total = None
            for u in range(3):
                part = None
                for v in range(3):
                    term = hid[row + u, j0 + v : j0 + v + 4, :, at] * taps[u * 3 + v, :, at][None]
                    part = term if part is None else part + term
                part = part.astype(F32)
                total = part if total is None else total + part
            total = total + depth_b[:, at][None]
            mid[j0 * 16 : j0 * 16 + 64, at] = gelu_bf16(total).reshape(64, 256)
    put_halves(moved, slice(0, 128), dot(mid[...], project_w[...]))
    base = img[row].astype(F32)
    for s in range(16):
        value = strided(moved, s, 8, 16) + base[s * 8 : s * 8 + 8]
        conv[slot, s, pl.ds(pl.multiple_of(r * 8, 8), 8), :] = value


def whole_wait(buf, chunk, sem):
    part = buf.at[chunk, pl.ds(0, PEERS)]
    pltpu.make_async_copy(part, part, sem.at[chunk]).wait()


def block_kernel(
    img, bn_gain, bn_shift, expand_w, expand_b, depth_k, depth_b, project_w,
    norm_gain, qkv_w, out_w, out,
    rowbuf, hid, mid, moved, conv, obuf, placed, rows_in, ends_out, ends_in, turned, taps,
    send, recv, reply, back, halo_sem, send_sem, recv_sem, reply_sem, back_sem,
):
    cols = lax.axis_size("col")
    me = lax.axis_index("row") * cols + lax.axis_index("col")
    barrier = pltpu.get_barrier_semaphore()

    def peer_of(o):
        return lax.rem(me + o, PEERS + 1)

    def place_of(peer):
        return (lax.div(peer, cols), lax.rem(peer, cols))

    def greet(o, _):
        pl.semaphore_signal(
            barrier, inc=1, device_id=place_of(peer_of(o)), device_id_type=pl.DeviceIdType.MESH
        )
        return 0

    lax.fori_loop(1, PEERS + 1, greet, 0)

    def scatter(chunk, src, dst, src_sem, dst_sem):
        def push(o, _):
            peer = peer_of(o)
            pltpu.make_async_remote_copy(
                src_ref=src.at[chunk, peer],
                dst_ref=dst.at[chunk, me],
                send_sem=src_sem.at[chunk],
                recv_sem=dst_sem.at[chunk],
                device_id=place_of(peer),
                device_id_type=pl.DeviceIdType.MESH,
            ).start()
            return 0

        lax.fori_loop(1, PEERS + 1, push, 0)
        dst[chunk, me] = src[chunk, me]

    my_row = lax.axis_index("row")
    my_col = lax.axis_index("col")
    row_count = lax.axis_size("row")
    pl.semaphore_wait(barrier, PEERS)

    def ring_copy(src, dst, sem, place):
        return pltpu.make_async_remote_copy(
            src_ref=src,
            dst_ref=dst,
            send_sem=halo_sem.at[sem],
            recv_sem=halo_sem.at[sem + 1],
            device_id=place,
            device_id_type=pl.DeviceIdType.MESH,
        )

    below = lax.rem(my_row + 1, row_count)
    above = lax.rem(my_row + row_count - 1, row_count)
    after = lax.rem(my_col + 1, cols)
    before = lax.rem(my_col + cols - 1, cols)
    down = ring_copy(img.at[31], rows_in.at[0], 0, (below, my_col))
    up = ring_copy(img.at[0], rows_in.at[1], 2, (above, my_col))
    down.start()
    up.start()
    chans = img.shape[2]
    for n in range(2):
        ends_out[n, 32:40, :] = jnp.zeros((8, chans), F32)
    for s in range(2):
        for n in range(2):
            part = qkv_w[s, :, n * 2 * chans : (n * 2 + 1) * chans]
            turned[s, n] = part.astype(F32).T.astype(BF16)
    for n in range(9):
        tap = depth_k[n // 3, n % 3 : n % 3 + 1, :]
        taps[n] = jnp.broadcast_to(tap.astype(F32), taps.shape[1:]).astype(BF16)
    for row in range(32):
        cells = img[row].astype(F32)
        ends_out[0, row + 1 : row + 2, :] = cells[:1]
        ends_out[1, row + 1 : row + 2, :] = cells[127:]
    down.wait()
    up.wait()
    for n, row in ((0, 0), (1, 33)):
        cells = rows_in[n].astype(F32)
        ends_out[0, row : row + 1, :] = cells[:1]
        ends_out[1, row : row + 1, :] = cells[127:]
    forth = ring_copy(ends_out.at[1], ends_in.at[0], 4, (my_row, after))
    aft = ring_copy(ends_out.at[0], ends_in.at[1], 6, (my_row, before))
    forth.start()
    aft.start()
    spot = lax.broadcasted_iota(jnp.int32, (16, chans), 0)
    edge_low = jnp.where((spot == 0) & (my_col == 0), 0.0, 1.0).astype(BF16)
    edge_high = jnp.where((spot == 15) & (my_col == cols - 1), 0.0, 1.0).astype(BF16)
    every = jnp.ones((16, chans), F32)
    edge_top = jnp.where(my_row == 0, 0.0, every).astype(BF16)
    edge_bottom = jnp.where(my_row == row_count - 1, 0.0, every).astype(BF16)
    forth.wait()
    aft.wait()

    def hide_row(row, cells, slot):
        hidden_row(
            row, cells, ends_in.at[0], ends_in.at[1], bn_gain, bn_shift, expand_w, expand_b, edge_low, edge_high,
            rowbuf.at[slot], hid,
        )

    def hide(i, _):
        for k in range(2):
            hide_row(2 * i + k + 1, img[2 * i + k], k)
        return 0

    lax.fori_loop(0, 16, hide, 0)
    hide_row(0, rows_in[0], 0)
    hide_row(33, rows_in[1], 1)
    for c in range(0, hid.shape[3], 256):
        hid[0, :, :, c : c + 256] = hid[0, :, :, c : c + 256] * edge_top[None]
        hid[33, :, :, c : c + 256] = hid[33, :, :, c : c + 256] * edge_bottom[None]

    def weights(s):
        return (
            norm_gain[s : s + 1, :],
            turned[s, 0],
            qkv_w[s, :, chans : 2 * chans],
            turned[s, 1],
            out_w[s],
        )

    def one_half(half, _):
        def mix(i, _):
            p = lax.div(i, 4)
            for k in range(2):
                mix_row(
                    p * 2 + half, lax.rem(i, 4) * 2 + k, p, img, taps, depth_b, project_w, hid,
                    mid.at[k], moved.at[k], conv,
                )
            return 0

        lax.fori_loop(0, 8, mix, 0)

        def attend_chunk(m, _):
            chunk = half * 4 + m
            x = jnp.concatenate([conv[w // 4, (w % 4) * 4 + m] for w in range(8)], axis=0)
            value = window_attend(x, *weights(0))
            put_halves(obuf, slice(0, 512), value)
            for d in range(PEERS + 1):
                block = [strided(obuf, 2 * d + e, 8, 64) for e in range(2)]
                send[chunk, d] = jnp.concatenate(block, axis=0).astype(BF16)
            scatter(chunk, send, recv, send_sem, recv_sem)
            return 0

        lax.fori_loop(0, 4, attend_chunk, 0)
        return 0

    lax.fori_loop(0, 2, one_half, 0)

    def grid_chunk(chunk, _):
        whole_wait(recv, chunk, recv_sem)
        blocks = recv[chunk].astype(F32)
        done = [
            set_attend(
                blocks[:, e * 8 : e * 8 + 8].reshape(256, 256), *weights(1)
            ).reshape(32, 8, 256)
            for e in range(2)
        ]
        reply[chunk] = jnp.concatenate(done, axis=1).astype(BF16)
        scatter(chunk, reply, back, reply_sem, back_sem)
        return 0

    lax.fori_loop(0, CHUNKS, grid_chunk, 0)

    def finish(chunk, _):
        whole_wait(back, chunk, back_sem)
        half = lax.div(chunk, 4)
        m = lax.rem(chunk, 4)
        put_halves(obuf, slice(0, 512), back[chunk].astype(F32).reshape(512, 256))
        for w in range(8):
            value = strided(obuf, w, 64, 8).reshape(8, 8, 256)
            rows = pl.ds((w // 4) * 16 + half * 8, 8)
            placed[rows, pl.ds(pl.multiple_of((w % 4) * 32 + m * 8, 8), 8), :] = value
        return 0

    def finish_half(half, _):
        lax.fori_loop(half * 4, half * 4 + 4, finish, 0)

        def store(i, _):
            row = lax.div(i, 8) * 16 + half * 8 + lax.rem(i, 8)
            out[row] = placed[row].astype(BF16)
            return 0

        lax.fori_loop(0, 16, store, 0)
        return 0

    lax.fori_loop(0, 2, finish_half, 0)

    def drain(chunk, _):
        whole_wait(send, chunk, send_sem)
        whole_wait(reply, chunk, reply_sem)
        return 0

    lax.fori_loop(0, CHUNKS, drain, 0)


PEERS = 31
CHUNKS = 8
VMEM = pl.BlockSpec(memory_space=pltpu.VMEM)


def per_device_fast(
    image, bn_gain, bn_shift, expand_weight, expand_bias, depth_kernel, depth_bias, project_weight,
    norm_gain, qkv_weight, out_weight,
):
    wide = expand_weight.shape[1]
    blocks = pltpu.VMEM((CHUNKS, PEERS + 1, 16, 256), BF16)
    sems = pltpu.SemaphoreType.DMA((CHUNKS,))
    return pl.pallas_call(
        block_kernel,
        out_shape=jax.ShapeDtypeStruct(image.shape, BF16),
        in_specs=[VMEM] * 11,
        out_specs=VMEM,
        scratch_shapes=[
            pltpu.VMEM((2, 2, 144, 128), F32),
            pltpu.VMEM((34, 10, 16, wide), BF16),
            pltpu.VMEM((2, 128, wide), BF16),
            pltpu.VMEM((2, 2, 128, 128), F32),
            pltpu.VMEM((2, 16, 64, 256), F32),
            pltpu.VMEM((2, 512, 128), F32),
            pltpu.VMEM(image.shape, F32),
            pltpu.VMEM((2, 128, 256), BF16),
            pltpu.VMEM((2, 40, 256), F32),
            pltpu.VMEM((2, 40, 256), F32),
            pltpu.VMEM((2, 2, 256, 256), BF16),
            pltpu.VMEM((9, 16, wide), BF16),
            blocks, blocks, blocks, blocks,
            sems, sems, sems, sems, sems,
        ],
        compiler_params=pltpu.CompilerParams(
            collective_id=0, has_side_effects=True, vmem_limit_bytes=56 * 1024 * 1024
        ),
    )(
        image, bn_gain[None], bn_shift[None], expand_weight, expand_bias[None],
        depth_kernel, depth_bias[None], project_weight, norm_gain, qkv_weight, out_weight,
    )


def solution(mesh):
    in_specs = (P("row", "col", None), P(), P(), P(), P(), P(), P(), P(), P(), P(), P())
    out_specs = P("row", "col", None)
    fast = mesh.shape["row"] == 8 and mesh.shape["col"] == 4
    return jax.shard_map(
        per_device_fast if fast else per_device, mesh=mesh, in_specs=in_specs, out_specs=out_specs, check_vma=False
    )
```
